256 devices in a mesh: ep: 8 (over z_hi, x), fsdp: 32 (over y, z_lo, core).
Axes of the slice: x: 4, y: 4, z: 8 (z_hi: 2, z_lo: 4; z = z_hi * 4 + z_lo), core: 2. Of those that a mesh axis runs over, the one named last changes fastest.
Arguments:
- tokens: bfloat16 [1024, 6144], P('ep', 'fsdp'), may hold values from -6 to 6
- expert_ids: int32 [1024, 2], P('ep'), may hold values from 0 to 7, all different within a row; in each aligned block of 128 rows (0 to 127, 128 to 255, ...) at most 64 rows name the same one
- combine_weights: float32 [1024, 2], P('ep'), may hold values from 0.25 to 1
- w_gate: bfloat16 [8, 6144, 8192], P('ep', None, 'fsdp'), may hold values from -0.078125 to 0.078125
- w_up: bfloat16 [8, 6144, 8192], P('ep', None, 'fsdp'), may hold values from -0.078125 to 0.078125
- w_down: bfloat16 [8, 8192, 6144], P('ep', 'fsdp'), may hold values from -0.0625 to 0.0625
Outputs:
- mixed_rows: bfloat16 [1024, 6144], P('ep', 'fsdp')
The draws below stay inside these ranges and needn't reach their ends.
Inputs may be any that keep to these rules, and one draw needn't show every extreme that they name: `expert_ids`: among the 128 tokens of one index of ep (aligned blocks of rows), no expert is named by more than 64 rows, a bound that some block reaches; a token names two different experts.
All inputs are finite; a program needn't handle non-finite values.
Results may differ from the reference program's by a relative error of at most 0.0057.
Values may be sent and summed in bfloat16 or wider, within the bound.
No kernel may reach another device: no remote copies, remote signals or barrier semaphores. Data moves between devices by JAX's collectives and lax.ppermute only.
A program may use at most 128 MiB of HBM per device.

```python
import math
import jax
import jax.numpy as jnp
import numpy as np
from jax import lax

D = 6144
FF = 8192
TOP = 2
TOK_EP = 128
EXPERTS = 8
CAP = 64
TOKENS = 1024
N_EP = 8


def block_levels(stream_key, shape, shards, least, high):
    loudness = 1.0
    for axis_at, parts in shards:
        heights = jax.random.uniform(jax.random.fold_in(jax.random.fold_in(stream_key, 6), axis_at), (parts,), jnp.float32, least / len(shards), high / len(shards))
        loudness = loudness * jnp.repeat(jnp.exp(heights), shape[axis_at] // parts).reshape((-1,) + (1,) * (len(shape) - 1 - axis_at))
    return loudness


def shared_out(rng, own, number, rows, number_of, top, reach, slope):
    order = jax.random.permutation(rng, number_of)
    heavy_load, common = portions_of(number_of, rows * top, reach, slope, True), portions_of(number_of, rows * top, reach, slope, False)
    places = jnp.arange(number_of)

    def named(lengths, rotation):
        used = int((lengths > 0).sum())
        fixed = max(1, used // 4)
        passed = fixed + (places - fixed + rotation * (used - fixed)) % max(1, number_of - fixed)
        return jnp.zeros((number_of,), jnp.int32).at[order[jnp.where(places < fixed, places, passed)]].set(jnp.asarray(lengths, jnp.int32))

    lengths = jnp.where(number % 4 == 0, named(heavy_load, number // 4), named(common, number - number // 4 - 1))
    mixed = jax.random.permutation(jax.random.fold_in(own, 3), number_of)
    source_of, receiver = mixed[0:number_of // 2 * 2:2], mixed[1:number_of // 2 * 2:2]
    room = jnp.minimum(lengths[source_of] - 1, reach - lengths[receiver]) // 2
    room = jnp.where((source_of == order[0]) | (receiver == order[0]) | (lengths[receiver] == 0), 0, jnp.maximum(room, 0))
    passed = jax.random.randint(jax.random.fold_in(own, 4), (number_of // 2,), 0, 1 << 20) % (room + 1)
    lengths = lengths.at[source_of].add(-passed).at[receiver].add(passed)
    labels = jnp.searchsorted(jnp.cumsum(lengths), jnp.arange(rows * top), side="right").astype(jnp.int32)
    listing = labels.reshape(top, rows).T
    listing = listing[jax.random.permutation(jax.random.fold_in(own, 1), rows)]
    rotation = jax.random.randint(jax.random.fold_in(own, 2), (rows, 1), 0, top)
    return jnp.take_along_axis(listing, (jnp.arange(top)[None, :] + rotation) % top, axis=1)


def portions_of(number_of, total, most, skew, full):
    portions = [(1 << 20) // math.isqrt(rank ** skew) + 1 for rank in range(1, number_of + 1)]
    largest = most if full else min(most, max(-(-total // number_of), total * portions[0] // sum(portions)))
    least = 1 if total - largest >= number_of - 1 else 0
    counts, spare = [largest] + [least] * (number_of - 1), total - largest - least * (number_of - 1)
    while spare > 0:
        candidates = [i for i in range(1, number_of) if counts[i] < largest] or [i for i in range(1, number_of) if counts[i] < most]
        pool, remaining = sum([portions[i] for i in candidates]), spare
        for i in candidates:
            addition = min(most - counts[i], max(1, remaining * portions[i] // pool), spare)
            counts[i] = counts[i] + addition
            spare = spare - addition
    return np.array(counts)


def normal_values(stream_key, dims, spread, bound, pieces=(), kind=jnp.bfloat16):
    drawn = jax.random.normal(stream_key, dims, jnp.float32) * spread
    if len(pieces) > 0:
        drawn = block_levels(stream_key, dims, pieces, -0.22, 0.18) * drawn
    return jnp.clip(drawn, min=-bound, max=bound).astype(kind)


def setup_inputs(seed: int = 0) -> dict:
    seeds = jax.random.split(jax.random.key(seed), 7)
    tokens = normal_values(seeds[0], (TOKENS, D), 1.0, 6.0, ((0, 8), (1, 32)))
    expert_ids_keys = jax.random.split(jax.random.fold_in(seeds[1], 1), TOKENS // TOK_EP)
    expert_ids_turns = jax.random.permutation(jax.random.fold_in(seeds[1], 3), TOKENS // TOK_EP)
    expert_ids = jax.vmap(lambda own, number: shared_out(jax.random.fold_in(seeds[1], 2), own, number, TOK_EP, EXPERTS, TOP, CAP, 2))(expert_ids_keys, expert_ids_turns).reshape((TOKENS, TOP))
    combine_weights = jnp.clip(0.25 + 0.75 * jax.random.uniform(seeds[2], (TOKENS, TOP), jnp.float32) ** block_levels(seeds[2], (TOKENS, TOP), ((0, 8),), -0.2, 0.2), 0.25, 1.0)
    w_gate = normal_values(seeds[3], (EXPERTS, D, FF), D ** -0.5, 0.078125, ((0, 8), (2, 32)))
    w_up = normal_values(seeds[4], (EXPERTS, D, FF), D ** -0.5, 0.078125, ((0, 8), (2, 32)))
    w_down = normal_values(seeds[5], (EXPERTS, FF, D), FF ** -0.5, 0.0625, ((0, 8), (1, 32)))
    return dict(tokens=tokens, expert_ids=expert_ids, combine_weights=combine_weights, w_gate=w_gate, w_up=w_up, w_down=w_down)


def place_rows(buffer, where, values):
    return buffer.at[where].set(values)


def run_expert(operands):
    expert_rows, gate_w, up_w, down_w = operands
    gate_sums = jnp.dot(expert_rows, gate_w, preferred_element_type=jnp.float32)
    up_sums = jnp.dot(expert_rows, up_w, preferred_element_type=jnp.float32)
    hidden = (jax.nn.silu(gate_sums) * up_sums).astype(jnp.bfloat16)
    return jnp.dot(hidden, down_w, preferred_element_type=jnp.float32).astype(jnp.bfloat16)


def reference(tokens, expert_ids, combine_weights, w_gate, w_up, w_down):
    model_width = tokens.shape[1]
    blocks = tokens.reshape(N_EP, TOK_EP, model_width)
    chosen = expert_ids.reshape(N_EP, TOK_EP * TOP).astype(jnp.int32)
    expert_lane = jnp.arange(EXPERTS, dtype=jnp.int32)
    onehot = (chosen[:, :, None] == expert_lane[None, None, :]).astype(jnp.int32)
    before = jnp.cumsum(onehot, axis=1, dtype=jnp.int32) - onehot
    slot_index = jnp.sum(before * onehot, axis=2).astype(jnp.int32)
    position = (chosen * CAP + slot_index).astype(jnp.int32)
    source_rows = jnp.repeat(blocks, TOP, axis=1)
    dispatched = jnp.zeros((N_EP, EXPERTS * CAP, model_width), tokens.dtype)
    dispatched = jax.vmap(place_rows)(dispatched, position, source_rows)
    per_expert = dispatched.reshape(N_EP, EXPERTS, CAP, model_width).transpose(1, 0, 2, 3)
    per_expert = per_expert.reshape(EXPERTS, N_EP * CAP, model_width)
    expert_out = lax.map(run_expert, (per_expert, w_gate, w_up, w_down))
    expert_out = expert_out.reshape(EXPERTS, N_EP, CAP, model_width)
    group_index = jnp.arange(N_EP, dtype=jnp.int32)[:, None]
    picked = expert_out[chosen, group_index, slot_index].astype(jnp.float32)
    picked = picked.reshape(N_EP, TOK_EP, TOP, model_width)
    scales = combine_weights.reshape(N_EP, TOK_EP, TOP)[..., None]
    mixed_rows = jnp.sum(picked * scales, axis=2)
    return mixed_rows.reshape(TOKENS, model_width).astype(jnp.bfloat16)
```

```python
import functools

import jax
import jax.numpy as jnp
from jax import lax
from jax.experimental import pallas as pl
from jax.experimental.pallas import tpu as pltpu
from jax.sharding import Mesh, PartitionSpec as P

SPLIT = ("zh", "x", "y", "zl", "c")
BF = jnp.bfloat16
F32 = jnp.float32
ZH, NX, NY, NZ = 2, 4, 4, 4
VMEM = 48 * 1024 * 1024


def shift(value, axis, size, by):
    return lax.ppermute(value, axis, [(i, (i + by) % size) for i in range(size)])


def swap(value):
    return lax.ppermute(value, "c", [(0, 1), (1, 0)])


def across(value, zh_by, x_by):
    pairs = []
    for h in range(ZH):
        for i in range(NX):
            there = (h + zh_by) % ZH * NX + (i + x_by) % NX
            pairs.append((h * NX + i, there))
    return lax.ppermute(value, ("zh", "x"), pairs)


def hidden_kernel(order, *refs):
    own, other = refs[:4], refs[4:8]
    wg, wu, hid, gate, up = refs[8:]
    k = pl.program_id(0)

    @pl.when(k == 0)
    def _():
        gate[...] = jnp.zeros_like(gate)
        up[...] = jnp.zeros_like(up)

    for o in range(4):

        @pl.when(k // 4 == o)
        def _():
            rows = jnp.concatenate([own[o][k % 4], other[o][k % 4]], axis=0)
            gate[...] += jnp.dot(rows, wg[0], preferred_element_type=F32)
            up[...] += jnp.dot(rows, wu[0], preferred_element_type=F32)

    @pl.when(k == 15)
    def _():
        g = gate[...]
        hid[...] = (g / (1.0 + jnp.exp(-g)) * up[...]).astype(BF)


def hidden_of(order, own, other, w_gate, w_up):
    _, rows, width = own[0].shape
    units = w_gate.shape[2]
    whole = pl.BlockSpec((4, rows, width), lambda k, s: (0, 0, 0))
    weight = pl.BlockSpec((1, width, units), lambda k, s: (0, s[k], 0))
    return pl.pallas_call(
        hidden_kernel,
        grid_spec=pltpu.PrefetchScalarGridSpec(
            num_scalar_prefetch=1,
            grid=(16,),
            in_specs=[whole] * 8 + [weight] * 2,
            out_specs=pl.BlockSpec((2 * rows, units), lambda k, s: (0, 0)),
            scratch_shapes=[pltpu.VMEM((2 * rows, units), F32)] * 2,
        ),
        out_shape=jax.ShapeDtypeStruct((2 * rows, units), BF),
        compiler_params=pltpu.CompilerParams(vmem_limit_bytes=VMEM),
        cost_estimate=pl.CostEstimate(
            flops=2 * 2 * rows * units * 2 * 16 * width,
            bytes_accessed=16 * width * (units * 4 + 4 * rows),
            transcendentals=2 * rows * units,
        ),
    )(order, *own, *other, w_gate, w_up)


def down_kernel(adds, order, hid, wd, *refs):
    k = pl.program_id(0)
    part = jnp.dot(hid[...], wd[0], preferred_element_type=F32)
    ins, outs = (refs[:4], refs[4:]) if adds else (None, refs)
    for o in range(4):

        @pl.when(k // 4 == o)
        def _():
            if adds:
                outs[o][0] = (part + ins[o][0].astype(F32)).astype(BF)
            else:
                outs[o][0] = part.astype(BF)


def down_of(order, hidden, half, w_down, arrived):
    rows2, units = hidden.shape
    rows = rows2 // 2
    width = w_down.shape[2] // 16
    lane = [
        pl.BlockSpec((1, rows, width), lambda k, s, o=o: (jnp.clip(k - 4 * o, 0, 3), 0, 0))
        for o in range(4)
    ]
    return pl.pallas_call(
        functools.partial(down_kernel, bool(arrived)),
        grid_spec=pltpu.PrefetchScalarGridSpec(
            num_scalar_prefetch=1,
            grid=(16,),
            in_specs=[
                pl.BlockSpec((rows, units), lambda k, s: (half, 0)),
                pl.BlockSpec((1, units, width), lambda k, s: (0, 0, s[k])),
            ]
            + (lane if arrived else []),
            out_specs=lane,
        ),
        out_shape=[jax.ShapeDtypeStruct((4, rows, width), BF)] * 4,
        compiler_params=pltpu.CompilerParams(vmem_limit_bytes=VMEM),
        cost_estimate=pl.CostEstimate(
            flops=2 * rows * units * 16 * width,
            bytes_accessed=16 * width * (units * 2 + 4 * rows),
            transcendentals=0,
        ),
    )(order, hidden, w_down, *arrived)


def flow(rows, order, outer, inner, w_gate, w_up, w_down):
    spread = [rows] + [shift(rows, inner, 4, i) for i in range(1, 4)]
    bundle = jnp.stack(spread)
    own = [bundle] + [shift(bundle, outer, 4, o) for o in range(1, 4)]
    other = [swap(v) for v in own]
    hidden = hidden_of(order, own, other, w_gate, w_up)
    sent = down_of(order, hidden, 1, w_down, [])
    arrived = [swap(v) for v in sent]
    paired = down_of(order, hidden, 0, w_down, arrived)
    met = [paired[0]] + [shift(paired[o], outer, 4, -o) for o in range(1, 4)]
    parts = [
        sum(m[i].astype(F32) for m in met) for i in range(4)
    ]
    last = [shift(parts[i].astype(BF), inner, 4, -i).astype(F32) for i in range(1, 4)]
    return (parts[0] + last[0] + last[1] + last[2]).astype(BF)


def shards(tokens, expert_ids, combine_weights, w_gate, w_up, w_down):
    zh, x, y, zl, c = (lax.axis_index(a) for a in SPLIT)
    tok_rows, width_local = tokens.shape
    experts = ZH * NX
    capacity = min(tok_rows, 4 * tok_rows // experts)
    half = capacity // 2
    beside = swap(tokens)
    chip_tokens = jnp.concatenate(
        [jnp.where(c == 0, tokens, beside), jnp.where(c == 0, beside, tokens)], axis=1
    )
    chosen = expert_ids.reshape(-1)
    n = chosen.shape[0]
    onehot = chosen[:, None] == jnp.arange(experts, dtype=jnp.int32)[None, :]
    earlier = jnp.arange(n)[:, None] > jnp.arange(n)[None, :]
    before = jnp.dot(earlier.astype(BF), onehot.astype(BF), preferred_element_type=F32)
    slot = jnp.sum(jnp.where(onehot, before, 0.0), axis=1).astype(jnp.int32)
    away = ((chosen // NX) ^ zh) * NX + (chosen % NX - x + NX) % NX
    place = jnp.where(slot // half == c, away * half + slot % half, -1).reshape(tok_rows, 2)
    places = jnp.arange(experts * half, dtype=jnp.int32)
    select = place[:, :, None] == places[None, None, :]
    dispatch = jnp.any(select, axis=1).astype(BF)
    packed = lax.dot_general(
        dispatch, chip_tokens, (((0,), (0,)), ((), ())), preferred_element_type=F32
    ).astype(BF)
    packed = packed.reshape(experts, half, 2 * width_local)

    zy = jnp.stack([((y - o) % NY) * NZ + (zl - i) % NZ for o in range(4) for i in range(4)])
    returned = []
    for h in range(ZH):
        sets = [packed[h * NX + i] for i in range(NX)]
        got = [s if (h, i) == (0, 0) else across(s, h, i) for i, s in enumerate(sets)]
        rows = jnp.concatenate(got, axis=0)
        out = flow(rows, zy, "y", "zl", w_gate, w_up, w_down)
        outs = [out[i * half : (i + 1) * half] for i in range(NX)]
        returned += [s if (h, i) == (0, 0) else across(s, h, -i) for i, s in enumerate(outs)]
    back = jnp.concatenate(returned, axis=0)
    weighting = jnp.sum(jnp.where(select, combine_weights[:, :, None], 0.0), axis=1)
    mixed = jnp.dot(weighting, back.astype(F32), precision=lax.Precision.HIGHEST)
    low, high = mixed[:, :width_local], mixed[:, width_local:]
    mine = jnp.where(c == 0, low, high)
    theirs = swap(jnp.where(c == 0, high, low))
    return (mine + theirs).astype(BF)


def solution(mesh):
    split = Mesh(mesh.devices.reshape(ZH, NX, NY, NZ, 2), SPLIT)
    ep, fsdp = ("zh", "x"), ("y", "zl", "c")
    in_specs = (
        P(ep, fsdp),
        P(ep, None),
        P(ep, None),
        P(ep, None, fsdp),
        P(ep, None, fsdp),
        P(ep, fsdp, None),
    )
    return jax.shard_map(
        shards, mesh=split, in_specs=in_specs, out_specs=P(ep, fsdp), check_vma=False
    )
```

```python
import functools

import jax
import jax.numpy as jnp
from jax import lax
from jax.experimental import pallas as pl
from jax.experimental.pallas import tpu as pltpu
from jax.sharding import Mesh, PartitionSpec as P

SPLIT = ("zh", "x", "y", "zl", "c")
BF = jnp.bfloat16
F32 = jnp.float32
ZH, NX, NY, NZ = 2, 4, 4, 4
VMEM = 40 * 1024 * 1024
PARAMS = pltpu.CompilerParams(vmem_limit_bytes=VMEM)


def shift(value, axis, by):
    return lax.ppermute(value, axis, [(i, (i + by) % 4) for i in range(4)])


def swap(value):
    return lax.ppermute(value, "c", [(0, 1), (1, 0)])


def across(value, x_by):
    pairs = []
    for h in range(ZH):
        for i in range(NX):
            pairs.append((h * NX + i, (1 - h) * NX + (i + x_by) % NX))
    return lax.ppermute(value, ("zh", "x"), pairs)


def call(kernel, grid, prefetch, ins, in_specs, out_shape, out_specs, scratch=(), flops=0, moved=0):
    return pl.pallas_call(
        kernel,
        grid_spec=pltpu.PrefetchScalarGridSpec(
            num_scalar_prefetch=1,
            grid=grid,
            in_specs=in_specs,
            out_specs=out_specs,
            scratch_shapes=list(scratch),
        ),
        out_shape=out_shape,
        compiler_params=PARAMS,
        cost_estimate=pl.CostEstimate(flops=flops, bytes_accessed=moved, transcendentals=0),
    )(prefetch, *ins)


def whole(shape):
    return pl.BlockSpec(shape, lambda k, s: (0,) * len(shape))


def route_kernel(half, where, ids, scales, dispatch, weighting):
    c, x, zh = where[8], where[9], where[10]
    tok = ids.shape[1]
    experts = ZH * NX
    lanes = lax.broadcasted_iota(jnp.int32, (experts, tok), 0)
    hot = [(ids[k : k + 1, :] == lanes).astype(F32) for k in range(2)]
    earlier = lax.broadcasted_iota(jnp.int32, (tok, tok), 0) < lax.broadcasted_iota(
        jnp.int32, (tok, tok), 1
    )
    before = jnp.dot(
        (hot[0] + hot[1]).astype(BF), earlier.astype(F32).astype(BF), preferred_element_type=F32
    )
    places = lax.broadcasted_iota(jnp.int32, (experts * half, tok), 0)
    weights = jnp.zeros((experts * half, tok), F32)
    taken = jnp.zeros((experts * half, tok), F32)
    for k in range(2):
        slot = jnp.sum(hot[k] * before, axis=0, keepdims=True).astype(jnp.int32)
        chosen = ids[k : k + 1, :]
        side = jnp.where(chosen >= NX, 1, 0)
        column = chosen - side * NX - x
        column = jnp.where(column < 0, column + NX, column)
        away = jnp.where(side == zh, 0, NX) + column
        inside = slot - c * half
        place = jnp.where((inside >= 0) & (inside < half), away * half + inside, -1)
        match = places == place
        weights += jnp.where(match, scales[k : k + 1, :], 0.0)
        taken += jnp.where(match, 1.0, 0.0)
    dispatch[...] = taken.astype(BF)
    weighting[...] = weights


def route(where, ids, scales, half):
    tok = ids.shape[1]
    n = ZH * NX * half
    return call(
        functools.partial(route_kernel, half),
        (1,),
        where,
        [ids, scales],
        [whole((2, tok))] * 2,
        [jax.ShapeDtypeStruct((n, tok), BF), jax.ShapeDtypeStruct((n, tok), F32)],
        [whole((n, tok))] * 2,
    )


def ordered(c, own, other):
    first = jnp.where(c == 0, own, other)
    second = jnp.where(c == 0, other, own)
    return jnp.concatenate([first, second], axis=0)


def spread_kernel(where, dispatch, *refs):
    own, other, outs = refs[:4], refs[4:8], refs[8:]
    step = pl.program_id(0)
    half = outs[0].shape[1]
    for o in range(4):

        @pl.when(step == o)
        def _():
            for i in range(4):
                rows = ordered(where[8], own[o][i], other[o][i])
                out = jnp.dot(dispatch[...], rows, preferred_element_type=F32).astype(BF)
                for e in range(4):
                    outs[e][i] = out[e * half : (e + 1) * half]


def spread_of(where, dispatch, own, other):
    n, tok = dispatch.shape
    _, part, width = own[0].shape
    half = n // 4
    return call(
        spread_kernel,
        (4,),
        where,
        [dispatch, *own, *other],
        [whole((n, tok))] + [whole((4, part, width))] * 8,
        [jax.ShapeDtypeStruct((16, half, width), BF)] * 4,
        [pl.BlockSpec((4, half, width), lambda k, s: (k, 0, 0))] * 4,
        flops=2 * n * tok * 16 * width,
        moved=16 * width * (tok + n) * 2,
    )


def hidden_kernel(pick, n, where, *refs):
    pieces, wg, wu = refs[:n], refs[n : n + 4], refs[n + 4 : n + 8]
    hid, gate, up = refs[n + 8 :]
    step = pl.program_id(0)

    @pl.when(step == 0)
    def _():
        gate[...] = jnp.zeros_like(gate)
        up[...] = jnp.zeros_like(up)

    def add(rows):
        g, u = gate[...], up[...]
        for i in range(4):
            g += jnp.dot(rows[i], wg[i][0], preferred_element_type=F32)
            u += jnp.dot(rows[i], wu[i][0], preferred_element_type=F32)
        gate[...] = g
        up[...] = u

    pick(step, pieces, add)

    @pl.when(step == 3)
    def _():
        g = gate[...]
        hid[...] = (g / (1.0 + jnp.exp(-g)) * up[...]).astype(BF)


def pick_by_group(step, pieces, add):
    add([jnp.concatenate([p[i] for p in pieces], axis=0) for i in range(4)])


def pick_by_outer(step, pieces, add):
    for o in range(4):

        @pl.when(step == o)
        def _():
            add([jnp.concatenate([pieces[o][i], pieces[4 + o][i]], axis=0) for i in range(4)])


def row_block(o_first, width, units):
    return [
        pl.BlockSpec((1, width, units), lambda k, s, i=i: (0, s[k] * 4 + s[4 + i], 0))
        for i in range(4)
    ]


def column_block(width, units):
    return [
        pl.BlockSpec((1, units, width), lambda k, s, i=i: (0, 0, s[k] * 4 + s[4 + i]))
        for i in range(4)
    ]


def hidden_of(where, pieces, w_gate, w_up, by_group):
    _, part, width = pieces[0].shape
    units = w_gate.shape[2]
    rows = part * (8 if by_group else 2)
    if by_group:
        spec, pick = pl.BlockSpec((4, part, width), lambda k, s: (k, 0, 0)), pick_by_group
    else:
        spec, pick = whole((4, part, width)), pick_by_outer
    return call(
        functools.partial(hidden_kernel, pick, 8),
        (4,),
        where,
        [*pieces, *[w_gate] * 4, *[w_up] * 4],
        [spec] * 8 + row_block(0, width, units) * 2,
        jax.ShapeDtypeStruct((rows, units), BF),
        whole((rows, units)),
        [pltpu.VMEM((rows, units), F32)] * 2,
        flops=2 * rows * units * 2 * 16 * width,
        moved=16 * width * (units * 4 + 2 * rows),
    )


def down_kernel(adds, by_group, where, hid, *refs):
    wd, refs = refs[:4], refs[4:]
    ins, outs = (refs[:4], refs[4:]) if adds else (None, refs)
    step = pl.program_id(0)

    def put(n, i, value):
        if adds:
            value = value + ins[n][i].astype(F32)
        outs[n][i] = value.astype(BF)

    for i in range(4):
        part = jnp.dot(hid[...], wd[i][0], preferred_element_type=F32)
        if by_group:
            half = outs[0].shape[1]
            for e in range(4):
                put(e, i, part[e * half : (e + 1) * half])
        else:
            for o in range(4):

                @pl.when(step == o)
                def _():
                    put(o, i, part)


def down_of(where, hidden, half, w_down, arrived, by_group):
    rows2, units = hidden.shape
    rows = rows2 // 2
    width = w_down.shape[2] // 16
    if by_group:
        shape = (16, rows // 4, width)
        lane = pl.BlockSpec((4, rows // 4, width), lambda k, s: (k, 0, 0))
    else:
        shape = (4, rows, width)
        lane = whole(shape)
    return call(
        functools.partial(down_kernel, bool(arrived), by_group),
        (4,),
        where,
        [hidden, *[w_down] * 4, *arrived],
        [pl.BlockSpec((rows, units), lambda k, s: (half, 0))]
        + column_block(width, units)
        + [lane] * len(arrived),
        [jax.ShapeDtypeStruct(shape, BF)] * 4,
        [lane] * 4,
        flops=2 * rows * units * 16 * width,
        moved=16 * width * (units * 2 + 4 * rows),
    )


def weigh_kernel(mine, adds, where, weighting, *refs):
    backs, refs = refs[:4], refs[4:]
    ins, outs = (refs[:4], refs[4:]) if adds else (None, refs)
    step = pl.program_id(0)
    w = weighting[...]
    high = w.astype(BF)
    middle = (w - high.astype(F32)).astype(BF)
    low = (w - high.astype(F32) - middle.astype(F32)).astype(BF)
    stack = jnp.concatenate([high, middle, low], axis=0)
    first = (where[8] == 0) == mine
    part = outs[0].shape[1]
    for i in range(4):
        rows = jnp.concatenate([b[i] for b in backs], axis=0)
        rows = jnp.concatenate([rows] * 3, axis=0)
        mixed = lax.dot_general(
            stack, rows, (((0,), (0,)), ((), ())), preferred_element_type=F32
        )
        value = jnp.where(first, mixed[:part], mixed[part:])
        for o in range(4):

            @pl.when(step == o)
            def _():
                outs[o][i] = (value + ins[o][i].astype(F32) if adds else value).astype(BF)


def weigh_of(where, weighting, backs, mine, arrived):
    n, tok = weighting.shape
    _, half, width = backs[0].shape
    shape = (4, tok // 2, width)
    return call(
        functools.partial(weigh_kernel, mine, bool(arrived)),
        (4,),
        where,
        [weighting, *backs, *arrived],
        [whole((n, tok))]
        + [pl.BlockSpec((4, half, width), lambda k, s: (k, 0, 0))] * 4
        + [whole(shape)] * len(arrived),
        [jax.ShapeDtypeStruct(shape, BF)] * 4,
        [whole(shape)] * 4,
        flops=6 * n * tok * 16 * width,
        moved=16 * width * (tok + n) * 2,
    )


def gather_plane(value):
    bundle = jnp.stack([value] + [shift(value, "zl", i) for i in range(1, 4)])
    return [bundle] + [shift(bundle, "y", o) for o in range(1, 4)]


def reduce_plane(parts):
    met = [parts[0]] + [shift(parts[o], "y", -o) for o in range(1, 4)]
    sums = [sum(m[i].astype(F32) for m in met) for i in range(4)]
    last = [shift(sums[i].astype(BF), "zl", -i).astype(F32) for i in range(1, 4)]
    return sums[0] + last[0] + last[1] + last[2]


def shards(tokens, expert_ids, combine_weights, w_gate, w_up, w_down):
    zh, x, y, zl, c = (lax.axis_index(a) for a in SPLIT)
    tok_rows, width_local = tokens.shape
    experts = ZH * NX
    half = min(tok_rows, 4 * tok_rows // experts) // 2
    part = tok_rows // 2
    where = jnp.stack(
        [(y - o) % 4 for o in range(4)] + [(zl - i) % 4 for i in range(4)] + [c, x, zh]
    ).astype(jnp.int32)
    beside = swap(tokens)
    chip_tokens = jnp.concatenate(
        [jnp.where(c == 0, tokens, beside), jnp.where(c == 0, beside, tokens)], axis=1
    )
    dispatch, weighting = route(where, expert_ids.T, combine_weights.T, half)
    n = NX * half

    packed = jnp.dot(dispatch[n:], chip_tokens, preferred_element_type=F32).astype(BF)
    got = [across(packed[i * half : (i + 1) * half], i) for i in range(NX)]
    far_own = gather_plane(jnp.concatenate(got, axis=0))
    far_other = [swap(v) for v in far_own]

    tok_own = gather_plane(lax.dynamic_slice_in_dim(chip_tokens, c * part, part, axis=0))
    tok_other = [swap(v) for v in tok_own]
    sets = spread_of(where, dispatch[:n], tok_own, tok_other)
    near_own = [sets[0]] + [shift(sets[i], "x", i) for i in range(1, 4)]
    near_other = [swap(v) for v in near_own]

    near_hidden = hidden_of(where, near_own + near_other, w_gate, w_up, True)
    near_sent = down_of(where, near_hidden, 1, w_down, [], True)
    near_paired = down_of(
        where, near_hidden, 0, w_down, [swap(v) for v in near_sent], True
    )
    far_hidden = hidden_of(where, far_own + far_other, w_gate, w_up, False)
    far_sent = down_of(where, far_hidden, 1, w_down, [], False)
    far_paired = down_of(where, far_hidden, 0, w_down, [swap(v) for v in far_sent], False)

    near_back = [near_paired[0]] + [shift(near_paired[i], "x", -i) for i in range(1, 4)]
    theirs = weigh_of(where, weighting[:n], near_back, False, [])
    near_mixed = reduce_plane(
        weigh_of(where, weighting[:n], near_back, True, [swap(v) for v in theirs])
    )

    far_out = reduce_plane(far_paired).astype(BF)
    far_back = jnp.concatenate(
        [across(far_out[i * half : (i + 1) * half], -i) for i in range(NX)], axis=0
    )
    far_mixed = lax.dot_general(
        weighting[n:],
        far_back.astype(F32),
        (((0,), (0,)), ((), ())),
        precision=lax.Precision.HIGHEST,
    )
    zero = jnp.zeros_like(near_mixed)
    near_all = jnp.concatenate(
        [jnp.where(c == 0, near_mixed, zero), jnp.where(c == 0, zero, near_mixed)], axis=0
    )
    mixed = far_mixed + near_all
    low, high = mixed[:, :width_local], mixed[:, width_local:]
    mine = jnp.where(c == 0, low, high)
    return (mine + swap(jnp.where(c == 0, high, low))).astype(BF)


def solution(mesh):
    split = Mesh(mesh.devices.reshape(ZH, NX, NY, NZ, 2), SPLIT)
    ep, fsdp = ("zh", "x"), ("y", "zl", "c")
    in_specs = (
        P(ep, fsdp),
        P(ep, None),
        P(ep, None),
        P(ep, None, fsdp),
        P(ep, None, fsdp),
        P(ep, fsdp, None),
    )
    return jax.shard_map(
        shards, mesh=split, in_specs=in_specs, out_specs=P(ep, fsdp), check_vma=False
    )
```

```python
import functools

import jax
import jax.numpy as jnp
from jax import lax
from jax.experimental import pallas as pl
from jax.experimental.pallas import tpu as pltpu
from jax.sharding import Mesh, PartitionSpec as P

SPLIT = ("zh", "x", "y", "zl", "c")
BF = jnp.bfloat16
F32 = jnp.float32
ZH, NX, NY, NZ = 2, 4, 4, 4
PARAMS = pltpu.CompilerParams(vmem_limit_bytes=12 * 1024 * 1024)


def shift(value, axis, by):
    return lax.ppermute(value, axis, [(i, (i + by) % 4) for i in range(4)])


def swap(value):
    return lax.ppermute(value, "c", [(0, 1), (1, 0)])


def over(value, by):
    pairs = []
    for h in range(ZH):
        for i in range(NZ):
            for core in range(2):
                there = (1 - h) * NZ + (i + by[core]) % NZ
                pairs.append(((h * NZ + i) * 2 + core, there * 2 + core))
    return lax.ppermute(value, ("zh", "zl", "c"), pairs)


def lanes(value, axis, by):
    pairs = []
    for i in range(4):
        for core in range(2):
            if by[core] is not None:
                pairs.append((i * 2 + core, (i + by[core]) % 4 * 2 + core))
    return lax.ppermute(value, (axis, "c"), pairs)


def call(kernel, where, ins, out_shape, scratch=(), after=(), flops=0, moved=0):
    n = len(ins)

    def body(where_ref, *refs):
        kernel(where_ref, *refs[:n], *refs[n + len(after) :])

    vmem = pl.BlockSpec(memory_space=pltpu.VMEM)
    return pl.pallas_call(
        body,
        in_specs=[pl.BlockSpec(memory_space=pltpu.SMEM)]
        + [vmem] * n
        + [pl.BlockSpec(memory_space=pl.ANY)] * len(after),
        out_specs=jax.tree.map(lambda _: vmem, out_shape),
        out_shape=out_shape,
        scratch_shapes=list(scratch),
        compiler_params=PARAMS,
        cost_estimate=pl.CostEstimate(flops=flops, bytes_accessed=moved, transcendentals=0),
    )(where, *ins, *after)


def split3(w):
    high = w.astype(BF)
    middle = (w - high.astype(F32)).astype(BF)
    low = (w - high.astype(F32) - middle.astype(F32)).astype(BF)
    return jnp.concatenate([high, middle, low], axis=1)


def route_kernel(cap, where, ids, scales, near_d, far_d, near_w, far_w):
    c, x, zh = where[8], where[9], where[10]
    tok = ids.shape[1]
    experts = ZH * NX
    lanes = lax.broadcasted_iota(jnp.int32, (experts, tok), 0)
    hot = [(ids[k : k + 1, :] == lanes).astype(F32) for k in range(2)]
    earlier = lax.broadcasted_iota(jnp.int32, (tok, tok), 0) < lax.broadcasted_iota(
        jnp.int32, (tok, tok), 1
    )
    before = jnp.dot(
        (hot[0] + hot[1]).astype(BF), earlier.astype(F32).astype(BF), preferred_element_type=F32
    )
    for near, first, count, d_ref, w_ref in (
        (True, 0, NX, near_d, near_w),
        (False, 0, NX, far_d, None),
        (False, 2 * c, NX // 2, None, far_w),
    ):
        places = lax.broadcasted_iota(jnp.int32, (count * cap, tok), 0)
        weights = jnp.zeros((count * cap, tok), F32)
        taken = jnp.zeros((count * cap, tok), F32)
        for k in range(2):
            slot = jnp.sum(hot[k] * before, axis=0, keepdims=True).astype(jnp.int32)
            chosen = ids[k : k + 1, :]
            side = jnp.where(chosen >= NX, 1, 0)
            column = chosen - side * NX - x
            column = jnp.where(column < 0, column + NX, column) - first
            fits = (column >= 0) & (column < count)
            fits = fits & ((side == zh) if near else (side != zh))
            match = places == jnp.where(fits, column * cap + slot, -1)
            weights += jnp.where(match, scales[k : k + 1, :], 0.0)
            taken += jnp.where(match, 1.0, 0.0)
        if d_ref is not None:
            d_ref[...] = taken.astype(BF)
        if w_ref is not None:
            w_ref[...] = split3(jnp.transpose(weights))


def route(where, ids, scales, cap):
    tok = ids.shape[1]
    n = NX * cap
    shapes = [(n, tok), (n, tok), (tok, 3 * n), (tok, 3 * n // 2)]
    return call(
        functools.partial(route_kernel, cap),
        where,
        [ids, scales],
        [jax.ShapeDtypeStruct(s, BF) for s in shapes],
    )


def spread_kernel(where, dispatch, own, first, second, *outs):
    cap = outs[0].shape[1]
    c = where[8]

    def put(rows_ref, j):
        for i in range(4):
            out = jnp.dot(dispatch[...], rows_ref[i], preferred_element_type=F32).astype(BF)
            for e in range(4):
                outs[e][j * 4 + i] = out[e * cap : (e + 1) * cap]

    @pl.when(c == 0)
    def _():
        put(own, 0)
        put(first, 1)

    @pl.when(c == 1)
    def _():
        put(first, 0)
        put(second, 1)


def spread_of(where, dispatch, own, first, second, after=()):
    n, tok = dispatch.shape
    width = own.shape[2]
    return call(
        spread_kernel,
        where,
        [dispatch, own, first, second],
        [jax.ShapeDtypeStruct((8, n // 4, width), BF)] * 4,
        (),
        after,
        flops=2 * n * tok * 8 * width,
        moved=8 * width * (tok + n) * 2,
    )


def weight_offset(where, base, j, i, width):
    return pl.multiple_of((where[base + j] * 4 + where[4 + i]) * width, width)


def hidden_kernel(near, n, where, *refs):
    pieces, (wg, wu, hid, gate, up) = refs[:n], refs[n:]
    c = where[8]
    width = pieces[0].shape[2]
    base = 12 if near else 0
    gate[...] = jnp.zeros_like(gate)
    up[...] = jnp.zeros_like(up)

    def add(rows, step, at):
        g, u = gate[...], up[...]
        for i in range(4):
            joined = jnp.concatenate([r[at + i] for r in rows], axis=0)
            units = pl.ds(weight_offset(where, base, step, i, width), width)
            g += jnp.dot(joined, wg[0, units, :], preferred_element_type=F32)
            u += jnp.dot(joined, wu[0, units, :], preferred_element_type=F32)
        gate[...] = g
        up[...] = u

    if near:
        for step in range(4):
            add(pieces[:4] if step < 2 else pieces[4:], step, step % 2 * 4)
    else:
        own, first, second, first_other, second_other = pieces
        add([own], 0, 0)

        @pl.when(c == 0)
        def _():
            add([first], 1, 0)
            add([first_other], 2, 0)
            add([second_other], 3, 0)

        @pl.when(c == 1)
        def _():
            add([first_other], 1, 0)
            add([first], 2, 0)
            add([second], 3, 0)

    g = gate[...]
    hid[...] = (g / (1.0 + jnp.exp(-g)) * up[...]).astype(BF)


def hidden_of(where, pieces, w_gate, w_up, near, after=()):
    _, part, width = pieces[0].shape
    units = w_gate.shape[2]
    rows = part * (4 if near else 1)
    return call(
        functools.partial(hidden_kernel, near, len(pieces)),
        where,
        [*pieces, w_gate, w_up],
        jax.ShapeDtypeStruct((rows, units), BF),
        [pltpu.VMEM((rows, units), F32)] * 2,
        after,
        flops=2 * rows * units * 2 * 16 * width,
        moved=16 * width * (units * 4 + 2 * rows),
    )


def down_kernel(n, mine, adds, near, where, hid, wd, *refs):
    ins, outs = (refs[:n], refs[n:]) if adds else (None, refs)
    base = 12 if mine else 14
    width = outs[0].shape[2]

    def put(j, source, out):
        for i in range(4):
            units = pl.ds(weight_offset(where, base, j, i, width), width)
            value = jnp.dot(hid[...], wd[0, :, units], preferred_element_type=F32)
            if near:
                cap, at = out[0].shape[1], j * 4 + i
                for e in range(4):
                    some = value[e * cap : (e + 1) * cap]
                    out[e][at] = (some + source[e][at].astype(F32) if adds else some).astype(BF)
            else:
                out[i] = (value + source[i].astype(F32) if adds else value).astype(BF)

    for j in range(2):
        if near:
            put(j, ins, outs)
        elif not adds:
            put(j, None, outs[j])
        else:
            pl.when(where[8] == 1 - j)(lambda j=j: put(j, ins[j], outs[0]))
            pl.when(where[8] == j)(lambda j=j: put(j, ins[j], outs[1]))


def down_of(where, hidden, mine, w_down, arrived, near, after=()):
    rows, units = hidden.shape
    width = w_down.shape[2] // 16
    n = 4 if near else 2
    shape = (8, rows // 4, width) if near else (4, rows, width)
    return call(
        functools.partial(down_kernel, n, mine, bool(arrived), near),
        where,
        [hidden, w_down, *arrived],
        [jax.ShapeDtypeStruct(shape, BF)] * n,
        (),
        after,
        flops=2 * rows * units * 8 * width,
        moved=8 * width * (units * 2 + 4 * rows),
    )


def weigh_kernel(where, stack, *refs):
    backs, (first, second) = refs[:4], refs[4:]

    def put(j, out):
        for i in range(4):
            rows = jnp.concatenate([b[j * 4 + i] for b in backs], axis=0)
            rows = jnp.concatenate([rows] * 3, axis=0)
            out[i] = jnp.dot(stack[...], rows, preferred_element_type=F32).astype(BF)

    for j in range(2):
        pl.when(where[8] == 1 - j)(lambda j=j: put(j, first))
        pl.when(where[8] == j)(lambda j=j: put(j, second))


def weigh_of(where, stack, backs, after=()):
    tok, n3 = stack.shape
    _, cap, width = backs[0].shape
    return call(
        weigh_kernel,
        where,
        [stack, *backs],
        [jax.ShapeDtypeStruct((4, tok, width), BF)] * 2,
        (),
        after,
        flops=2 * n3 * tok * 8 * width,
        moved=8 * width * (tok + 4 * cap) * 2,
    )


def finish_kernel(where, stack, near, *refs):
    backs, out = refs[:2], refs[2]
    rows = jnp.concatenate([b[...] for b in backs], axis=0)
    rows = jnp.concatenate([rows] * 3, axis=0)
    mixed = jnp.dot(stack[...], rows, preferred_element_type=F32)
    out[...] = mixed + near[...]


def finish(where, stack, near, backs):
    tok, n3 = stack.shape
    width = backs[0].shape[1]
    return call(
        finish_kernel,
        where,
        [stack, near, *backs],
        jax.ShapeDtypeStruct((tok, width), F32),
        flops=2 * tok * n3 * width,
        moved=tok * width * 4,
    )


def mine_of(c, first, second):
    return jnp.where(c == 0, first, second)


def four(c, own, first, second):
    other, last = swap(first), lax.ppermute(second, "c", [(1, 0)])
    return jnp.stack(
        [own, mine_of(c, first, other), mine_of(c, other, first), mine_of(c, last, second)]
    )


def y_gather(line):
    return lanes(line, "y", (1, 2)), lanes(line, "y", (None, 3))


def y_sum(c, first, second, after):
    arrived = [lanes(first, "y", (-1, -2)), lanes(second, "y", (None, -3))]
    _, *arrived = lax.optimization_barrier((after, *arrived))
    return arrived[0].astype(F32) + mine_of(c, second, arrived[1]).astype(F32)


def halves_sum(c, met):
    sent = mine_of(c, met[2:], met[:2]).astype(BF)
    return mine_of(c, met[:2], met[2:]) + swap(sent).astype(F32)


def core_sum(c, met):
    part = met.shape[1] // 2
    kept = mine_of(c, met[:, :part], met[:, part:])
    return kept + swap(mine_of(c, met[:, part:], met[:, :part]).astype(BF)).astype(F32)


def shards(tokens, expert_ids, combine_weights, w_gate, w_up, w_down):
    zh, x, y, zl, c = (lax.axis_index(a) for a in SPLIT)
    tok_rows, width_local = tokens.shape
    cap = min(tok_rows, 4 * tok_rows // (ZH * NX))
    own_y = [(y - 2 * c - j) % 4 for j in range(4)]
    where = jnp.stack(
        [(y - o) % 4 for o in range(4)] + [(zl - i) % 4 for i in range(4)] + [c, x, zh, x] + own_y
    ).astype(jnp.int32)
    beside = swap(tokens)
    chip_tokens = jnp.concatenate(
        [mine_of(c, tokens, beside), mine_of(c, beside, tokens)], axis=1
    )
    near_d, far_d, near_w, far_w = route(where, expert_ids.T, combine_weights.T, cap)

    packed = jnp.dot(far_d, chip_tokens, preferred_element_type=F32).astype(BF)
    sets = [packed[i * cap : (i + 1) * cap] for i in range(NX)]
    sent = [shift(sets[i], "x", i) for i in range(1, 4)]

    line = [lanes(chip_tokens, "zl", (1, 2)), lanes(chip_tokens, "zl", (None, 3))]
    got = jnp.concatenate([sets[0]] + sent, axis=0)
    _, *line = lax.optimization_barrier((got, *line))
    line = four(c, chip_tokens, *line)
    sets = spread_of(where, near_d, line, *y_gather(line))
    near_own = [sets[0]] + [shift(sets[i], "x", i) for i in range(1, 4)]
    _, kept = lax.optimization_barrier((near_own[1], sets[0]))
    near_other = [swap(v) for v in [kept] + near_own[1:]]

    crossed = [over(got, (0, 2)), over(got, (1, 3))]
    _, *crossed = lax.optimization_barrier((sets, *crossed))
    pair = jnp.stack(crossed)
    other = swap(pair)
    bundle = jnp.concatenate([mine_of(c, pair, other), mine_of(c, other, pair)], axis=0)
    first, second = y_gather(bundle)
    far = [bundle, first, second, swap(first), lax.ppermute(second, "c", [(1, 0)])]

    near_hidden = hidden_of(where, near_own + near_other, w_gate, w_up, True, [first, second])
    far_hidden = hidden_of(where, far, w_gate, w_up, False, [near_hidden])
    far_sent = down_of(where, far_hidden, False, w_down, [], False)
    far_arrived = [swap(v) for v in far_sent]
    near_sent = down_of(where, near_hidden, False, w_down, [], True, far_sent[:1])
    near_arrived = [swap(v) for v in near_sent]
    far_paired = down_of(where, far_hidden, True, w_down, far_arrived, False, near_sent[:1])
    near_paired = down_of(where, near_hidden, True, w_down, near_arrived, True, far_paired[:1])
    near_back = [near_paired[0]] + [shift(near_paired[i], "x", -i) for i in range(1, 4)]

    met = y_sum(c, *far_paired, [near_back[1], near_back[3]])
    kept = halves_sum(c, met).astype(BF)
    home = [over(kept[0], (0, -2)), over(kept[1], (-1, -3))]
    near_met = y_sum(c, *weigh_of(where, near_w, near_back), home)

    home = home[0].astype(F32) + home[1].astype(F32)
    far_out = core_sum(c, home[None])[0].astype(BF)

    kept = halves_sum(c, near_met)
    one = lanes(mine_of(c, kept[1], kept[0]).astype(BF), "zl", (-1, -2))
    two = lanes(kept[1].astype(BF), "zl", (None, -3))
    near_mixed = mine_of(c, kept[0], two.astype(F32)) + one.astype(F32)

    low, high = far_out[:cap], far_out[cap:]
    one, two = lanes(mine_of(c, high, low), "x", (-1, -2)), lanes(high, "x", (None, -3))
    back = [mine_of(c, low, one), mine_of(c, one, two)]
    mixed = finish(where, far_w, near_mixed, back)
    low, high = mixed[:, :width_local], mixed[:, width_local:]
    return (mine_of(c, low, high) + swap(mine_of(c, high, low))).astype(BF)


def solution(mesh):
    split = Mesh(mesh.devices.reshape(ZH, NX, NY, NZ, 2), SPLIT)
    ep, fsdp = ("zh", "x"), ("y", "zl", "c")
    in_specs = (
        P(ep, fsdp),
        P(ep, None),
        P(ep, None),
        P(ep, None, fsdp),
        P(ep, None, fsdp),
        P(ep, fsdp, None),
    )
    return jax.shard_map(
        shards, mesh=split, in_specs=in_specs, out_specs=P(ep, fsdp), check_vma=False
    )
```
